32 devices in a mesh: groups: 2 (over x), dp: 8 (over z, core), tensor: 2 (over y).
Axes of the slice: x: 2, y: 2, z: 4, core: 2. Of those that a mesh axis runs over, the one named last changes fastest.
Arguments:
- tokens: bfloat16 [4096, 8192], P(('groups', 'dp'), 'tensor'), parts along dimension 0, may hold values from -260 to 260
- tenant_ids: int32 [16, 256], P(('groups', 'dp')), parts along dimension 0, may hold values from 0 to 7, never falling along the last dimension, each value on 1 to 64 neighbouring positions
- cot_query: bfloat16 [4096, 4096], P(('groups', 'dp'), 'tensor'), parts along dimension 0, may hold values from -6 to 6
- cot_value: bfloat16 [4096, 1024], P(('groups', 'dp'), 'tensor'), parts along dimension 0, may hold values from -6 to 6
- w_query: bfloat16 [8192, 4096], P(None, 'tensor'), may hold values from -0.0625 to 0.0625
- w_value: bfloat16 [8192, 1024], P(None, 'tensor'), may hold values from -0.0625 to 0.0625
- a_query: bfloat16 [8, 64, 8192], P('dp', None, 'tensor'), may hold values from -0.0625 to 0.0625
- a_value: bfloat16 [8, 64, 8192], P('dp', None, 'tensor'), may hold values from -0.0625 to 0.0625
- b_query: bfloat16 [8, 64, 4096], P('dp', None, 'tensor'), may hold values from -0.09375 to 0.09375
- b_value: bfloat16 [8, 64, 1024], P('dp', None, 'tensor'), may hold values from -0.1875 to 0.1875
Outputs:
- input_grad: bfloat16 [4096, 8192], P(('groups', 'dp'), 'tensor'), parts along dimension 0
- grad_a_query: float32 [16, 64, 8192], P(('groups', 'dp'), None, 'tensor'), parts along dimension 0
- grad_a_value: float32 [16, 64, 8192], P(('groups', 'dp'), None, 'tensor'), parts along dimension 0
- grad_b_query: float32 [16, 64, 4096], P(('groups', 'dp'), None, 'tensor'), parts along dimension 0
- grad_b_value: float32 [16, 64, 1024], P(('groups', 'dp'), None, 'tensor'), parts along dimension 0
The draws below stay inside these ranges and needn't reach their ends.
There are 2 independent parts, one for each index of `groups`. The reference program is written for one: setup_inputs(seed, part) draws one part's arguments, and reference() takes and returns one part's arrays. A program takes and returns all parts, laid end to end along the dimension named above; an argument that names none is the same for every part. Nothing has to cross between parts.
Inputs may be any that keep to these rules, and one draw needn't show every extreme that they name: `tenant_ids`: on each line of 256 rows the tenant ids never fall, every one of the 8 tenants holds 1 to 64 rows, and some tenant holds exactly 64.
All inputs are finite; a program needn't handle non-finite values.
Results may differ from the reference program's by a relative error of at most 0.017.
Values may be sent and summed in bfloat16 or wider, within the bound.
A program may use at most 192 MiB of HBM per device.

```python
import math
import jax
import jax.numpy as jnp
import numpy as np
from jax import lax

D = 8192
QW = 4096
KV = 1024
R = 64
TOK_DEV = 256
TEN = 8
MOST = 64
TOKENS = 2048
N_DP = 8
N_TENSOR = 2


def draw_tokens(key, part):
    key = jax.random.fold_in(key, 11)
    base_key, col_key, row_key = jax.random.split(key, 3)
    column = jnp.arange(D, dtype=jnp.float32)
    col_scale = 10.0 ** (column / D) * jax.random.uniform(col_key, (D,), jnp.float32, 0.6, 1.4)
    row_scale = jnp.exp(jax.random.uniform(row_key, (TOKENS, 1), jnp.float32, 0.0, 2.302585))
    base = jnp.clip(jax.random.normal(base_key, (TOKENS, D), jnp.float32), -6.0, 6.0)
    return (base * col_scale * row_scale * 0.3).astype(jnp.bfloat16)


def levels(own_key, shape, pieces, least, top_value):
    loudness, own = 1.0, jax.random.fold_in(own_key, 6)
    for axis_at, shards_of in pieces:
        heights = jnp.exp(jax.random.uniform(jax.random.fold_in(own, axis_at), (shards_of,), jnp.float32, least / len(pieces), top_value / len(pieces)))
        loudness = loudness * jnp.repeat(heights, shape[axis_at] // shards_of).reshape([-1 if axis == axis_at else 1 for axis in range(len(shape))])
    return loudness


def profile(count, total, most, lean):
    weights = [(1 << 20) // math.isqrt(rank ** lean) + 1 for rank in range(2, count + 1)]
    rest, given = total - most - (count - 1), [1] * (count - 1)
    while rest > 0:
        movable = [i for i in range(count - 1) if given[i] < most]
        pool, left = sum([weights[i] for i in movable]), rest
        for i in movable:
            more = min(most - given[i], max(1, left * weights[i] // pool), rest)
            given[i] = given[i] + more
            rest = rest - more
    return np.array([most] + given)


def ragged(own_key, amount, total, most, slope):
    if amount == 2:
        one = jax.random.randint(own_key, (), max(1, total - most), min(most, total - 1) + 1)
        return jnp.stack([one, total - one])
    sizes = jnp.asarray(profile(amount, total, most, slope), jnp.int32)
    pairs = (amount - 1) // 2
    source_of, receiver = sizes[1:1 + 2 * pairs:2], sizes[2:2 + 2 * pairs:2]
    slack = jnp.minimum(source_of - 1, most - receiver)
    moved = jax.random.randint(jax.random.fold_in(own_key, 1), (pairs,), 0, 1 << 20) % (slack + 1)
    sizes = sizes.at[1:1 + 2 * pairs:2].set(source_of - moved).at[2:2 + 2 * pairs:2].set(receiver + moved)
    return sizes[jax.random.permutation(jax.random.fold_in(own_key, 2), amount)]


def gaussian(own_key, shape, width, bound, cuts=(), kind=jnp.bfloat16):
    drawn = width * jax.random.normal(own_key, shape, jnp.float32)
    if cuts:
        drawn = drawn * levels(own_key, shape, cuts, -0.22, 0.18)
    return jnp.clip(drawn, -bound, bound).astype(kind)


def setup_inputs(seed: int = 0, part: int = 0) -> dict:
    key_list = jax.random.split(jax.random.key(seed), 11)
    part_splits = jax.random.split(jax.random.fold_in(key_list[10], part), 11)
    return {
        "tokens": draw_tokens(jax.random.fold_in(jax.random.fold_in(key_list[10], part), 71), part),
        "tenant_ids": jax.vmap(lambda own: jnp.searchsorted(jnp.cumsum(ragged(own, TEN, TOK_DEV, MOST, 2)), jnp.arange(TOK_DEV), side="right"))(jax.random.split(part_splits[1], N_DP)).reshape((N_DP, TOK_DEV)).astype(jnp.int32),
        "cot_query": gaussian(part_splits[2], (TOKENS, QW), 1.0, 6.0, ((0, 8), (1, 2))),
        "cot_value": gaussian(part_splits[3], (TOKENS, KV), 1.0, 6.0, ((0, 8), (1, 2))),
        "w_query": gaussian(key_list[4], (D, QW), D ** -0.5, 0.0625, ((1, 2),)),
        "w_value": gaussian(key_list[5], (D, KV), D ** -0.5, 0.0625, ((1, 2),)),
        "a_query": gaussian(key_list[6], (TEN, R, D), D ** -0.5, 0.0625, ((0, 8), (2, 2))),
        "a_value": gaussian(key_list[7], (TEN, R, D), D ** -0.5, 0.0625, ((0, 8), (2, 2))),
        "b_query": gaussian(key_list[8], (TEN, R, QW), QW ** -0.5, 0.09375, ((0, 8), (2, 2))),
        "b_value": gaussian(key_list[9], (TEN, R, KV), KV ** -0.5, 0.1875, ((0, 8), (2, 2))),
    }


SCALE = 2.0
CLIP_RMS = 0.5

def reference(tokens, tenant_ids, cot_query, cot_value, w_query, w_value, a_query, a_value, b_query, b_value):
    tenant_row = tenant_ids.reshape(-1)
    tenants, rank_dim, feat_width = a_query.shape
    flat_aq = a_query.reshape(tenants * rank_dim, feat_width)
    flat_av = a_value.reshape(tenants * rank_dim, feat_width)
    flat_bq = b_query.reshape(tenants * rank_dim, QW)
    flat_bv = b_value.reshape(tenants * rank_dim, KV)
    sum_hq = jnp.dot(tokens, flat_aq.T, preferred_element_type=jnp.float32)
    sum_hv = jnp.dot(tokens, flat_av.T, preferred_element_type=jnp.float32)
    sum_gq = jnp.dot(cot_query, flat_bq.T, preferred_element_type=jnp.float32)
    sum_gv = jnp.dot(cot_value, flat_bv.T, preferred_element_type=jnp.float32)
    column_tenant = jnp.arange(tenants * rank_dim, dtype=jnp.int32) // rank_dim
    row_mask = (tenant_row[:, None] == column_tenant[None, :]).astype(jnp.float32)
    masked_hq = (sum_hq * row_mask).astype(jnp.bfloat16)
    masked_hv = (sum_hv * row_mask).astype(jnp.bfloat16)
    masked_gq = (sum_gq * row_mask).astype(jnp.bfloat16)
    masked_gv = (sum_gv * row_mask).astype(jnp.bfloat16)
    query_block = QW // N_TENSOR
    value_block = KV // N_TENSOR
    frozen = jnp.zeros((tokens.shape[0], feat_width), jnp.float32)
    for shard_idx in range(N_TENSOR):
        q_lo = shard_idx * query_block
        v_lo = shard_idx * value_block
        partial_term = jnp.dot(cot_query[:, q_lo:q_lo + query_block], w_query[:, q_lo:q_lo + query_block].T, preferred_element_type=jnp.float32)
        partial_term = partial_term + jnp.dot(cot_value[:, v_lo:v_lo + value_block], w_value[:, v_lo:v_lo + value_block].T, preferred_element_type=jnp.float32)
        rounded = lax.optimization_barrier(partial_term.astype(jnp.bfloat16))
        frozen = frozen + rounded.astype(jnp.float32)
    adapter_term = jnp.dot(masked_gq, flat_aq, preferred_element_type=jnp.float32) + jnp.dot(masked_gv, flat_av, preferred_element_type=jnp.float32)
    input_grad = (frozen + SCALE * adapter_term).astype(jnp.bfloat16)
    raw_aq = SCALE * jnp.dot(masked_gq.T, tokens, preferred_element_type=jnp.float32).reshape(tenants, rank_dim, feat_width)
    raw_av = SCALE * jnp.dot(masked_gv.T, tokens, preferred_element_type=jnp.float32).reshape(tenants, rank_dim, feat_width)
    raw_bq = SCALE * jnp.dot(masked_hq.T, cot_query, preferred_element_type=jnp.float32).reshape(tenants, rank_dim, QW)
    raw_bv = SCALE * jnp.dot(masked_hv.T, cot_value, preferred_element_type=jnp.float32).reshape(tenants, rank_dim, KV)
    norm_sq = lax.optimization_barrier(jnp.sum(raw_aq * raw_aq, axis=(1, 2))) + lax.optimization_barrier(jnp.sum(raw_av * raw_av, axis=(1, 2)))
    norm_sq = norm_sq + lax.optimization_barrier(jnp.sum(raw_bq * raw_bq, axis=(1, 2))) + lax.optimization_barrier(jnp.sum(raw_bv * raw_bv, axis=(1, 2)))
    entries = float(R * (2 * D + QW + KV))
    factor = jnp.minimum(1.0, CLIP_RMS * jnp.sqrt(entries) / jnp.sqrt(norm_sq + 1e-06))[:, None, None]
    return (input_grad, raw_aq * factor, raw_av * factor, raw_bq * factor, raw_bv * factor)
```

```python
import functools
import math

import jax
import jax.numpy as jnp
from jax import lax
from jax.experimental import pallas as pl
from jax.experimental.pallas import tpu as pltpu
from jax.sharding import PartitionSpec as P

D = 8192
QW = 4096
KV = 1024
R = 64

SCALE = 2.0
CLIP_RMS = 0.5
MESH = pl.DeviceIdType.MESH
PIECE = 16


def dot_cols(left, right):
    return lax.dot_general(
        left, right, (((1,), (1,)), ((), ())), preferred_element_type=jnp.float32
    )


def remote(src, dst, send, recv, where):
    return pltpu.make_async_remote_copy(
        src_ref=src, dst_ref=dst, send_sem=send, recv_sem=recv, device_id=where, device_id_type=MESH
    )


def greet(z, nz, pairs, t, nt, x_partner):
    barrier = pltpu.get_barrier_semaphore()

    def signal(where):
        pl.semaphore_signal(barrier, inc=1, device_id=where, device_id_type=MESH)

    left, right, core = pairs

    @pl.when(z > 0)
    def _():
        signal({"dp": left})

    @pl.when(z < nz - 1)
    def _():
        signal({"dp": right})

    signal({"dp": core})
    if x_partner is not None:
        signal({"groups": x_partner})
    for d in range(nt - 1):
        signal({"tensor": lax.rem(t + 1 + d, nt)})
    always = 1 + (x_partner is not None) + nt - 1
    ends = jnp.where(z > 0, 1, 0) + jnp.where(z < nz - 1, 1, 0)
    pl.semaphore_wait(barrier, always + ends)


def gather_kernel(
    n_dp, nt, tile,
    mine, cq, cv, wq, wv,
    full, frozen, parts,
    wq_buf, wv_buf, out_buf,
    w_sem, l_sem, own_send, own_recv, z_send, z_recv, x_send, x_recv, c_send, c_recv,
    p_send, p_recv,
):
    nz = n_dp // 2
    me = lax.axis_index("dp")
    g = lax.axis_index("groups")
    t = lax.axis_index("tensor")
    z, c = me // 2, lax.rem(me, 2)
    other = 1 - g
    core = 2 * z + 1 - c
    left, right = me - 2, me + 2
    half = R // 2
    npiece = half // PIECE

    def rows(which, p):
        return pl.ds(pl.multiple_of(which * half + p * PIECE, PIECE), PIECE)

    def tiles(i, slot):
        per = frozen.shape[1] // tile
        peer = lax.rem(t + 1 + i // per, nt)
        at = pl.ds(pl.multiple_of(peer * frozen.shape[1] + lax.rem(i, per) * tile, tile), tile)
        return (
            pltpu.make_async_copy(wq.at[at], wq_buf.at[slot], w_sem.at[0, slot]),
            pltpu.make_async_copy(wv.at[at], wv_buf.at[slot], w_sem.at[1, slot]),
        )

    for copy in tiles(0, 0):
        copy.start()

    greet(z, nz, (left, right, core), t, nt, other)

    def z_copy(way, k, p, source):
        slot = 2 * (z - k if way == 0 else z + k) + c
        at = rows(g, p)
        src = mine.at[at] if source else full.at[slot, at]
        return remote(
            src, full.at[slot, at], z_send.at[way, k, p], z_recv.at[way, k, p],
            {"dp": right if way == 0 else left},
        )

    def z_arrival(way, k, p):
        slot = 2 * (z - k - 1 if way == 0 else z + k + 1) + c
        at = full.at[slot, rows(g, p)]
        return remote(
            at, at, z_send.at[way, k, p], z_recv.at[way, k, p],
            {"dp": right if way == 0 else left},
        )

    def x_copy(way, k, p, arriving):
        slot = 2 * (z - k - 1 if way == 0 else z + k + 1) + c
        at = full.at[slot, rows(other if arriving else g, p)]
        return remote(at, at, x_send.at[way, k, p], x_recv.at[way, k, p], {"groups": other})

    def c_copy(which, way, k, p, arriving):
        slot = 2 * (z - k - 1 if way == 0 else z + k + 1) + (1 - c if arriving else c)
        at = full.at[slot, rows(g if which == 0 else other, p)]
        return remote(
            at, at, c_send.at[which, way, k, p], c_recv.at[which, way, k, p], {"dp": core}
        )

    def sends(way, k):
        if way == 0:
            return jnp.logical_and(z - k >= 0, z < nz - 1)
        return jnp.logical_and(z + k <= nz - 1, z > 0)

    def gets(way, k):
        return z - k - 1 >= 0 if way == 0 else z + k + 1 <= nz - 1

    for p in range(npiece):
        for way in range(2):
            @pl.when(sends(way, 0))
            def _(way=way, p=p):
                z_copy(way, 0, p, True).start()

    local = pltpu.make_async_copy(mine, full.at[me], l_sem)
    local.start()
    own = remote(mine, full.at[me], own_send, own_recv, {"dp": core})
    own.start()
    own_in = remote(mine, full.at[core], own_send, own_recv, {"dp": core})

    per = frozen.shape[1] // tile
    total, away = nt * per, (nt - 1) * per

    def p_copy(i):
        at = pl.ds(pl.multiple_of(lax.rem(i, per) * tile, tile), tile)
        peer = lax.rem(t + 1 + i // per, nt)
        return remote(
            out_buf.at[i], parts.at[i // per, :, at], p_send.at[i], p_recv.at[i], {"tensor": peer}
        )

    def step(i, carry):
        slot = lax.rem(i, 2)
        for copy in tiles(i, slot):
            copy.wait()

        @pl.when(i + 1 < total)
        def _():
            for copy in tiles(i + 1, 1 - slot):
                copy.start()

        value = dot_cols(cq[...], wq_buf[slot]) + dot_cols(cv[...], wv_buf[slot])
        value = value.astype(jnp.bfloat16)

        @pl.when(i < away)
        def _():
            out_buf[i] = value
            p_copy(i).start()

        @pl.when(i >= away)
        def _():
            at = pl.ds(pl.multiple_of(lax.rem(i, per) * tile, tile), tile)
            frozen[:, at] = value

        return carry

    lax.fori_loop(0, total, step, 0)

    def from_x(k):
        for p in range(npiece):
            for way in range(2):
                @pl.when(gets(way, k))
                def _(way=way, p=p):
                    x_copy(way, k, p, True).wait_recv()
                    c_copy(1, way, k, p, False).start()

    for k in range(nz - 1):
        for p in range(npiece):
            for way in range(2):
                @pl.when(gets(way, k))
                def _(way=way, p=p, k=k):
                    z_arrival(way, k, p).wait_recv()
                    if k + 1 < nz - 1:
                        @pl.when(sends(way, k + 1))
                        def _():
                            z_copy(way, k + 1, p, False).start()
                    x_copy(way, k, p, False).start()
                    c_copy(0, way, k, p, False).start()
        if k > 0:
            from_x(k - 1)
    from_x(nz - 2)

    own_in.wait_recv()
    for k in range(nz - 1):
        for p in range(npiece):
            for way in range(2):
                @pl.when(gets(way, k))
                def _(way=way, p=p, k=k):
                    for which in range(2):
                        c_copy(which, way, k, p, True).wait_recv()
                        c_copy(which, way, k, p, False).wait_send()
                    x_copy(way, k, p, False).wait_send()

                @pl.when(sends(way, k))
                def _(way=way, p=p, k=k):
                    z_copy(way, k, p, k == 0).wait_send()
    own.wait_send()
    local.wait()

    def finish(i, carry):
        p_copy(i).wait_recv()
        p_copy(i).wait_send()
        return carry

    lax.fori_loop(0, away, finish, 0)


def gather(mine, cq, cv, wq, wv, n_dp, nt):
    rank, width = mine.shape
    rows = cq.shape[0]
    feat = wq.shape[0] // nt
    tile = min(512, feat)
    nz = n_dp // 2
    npiece = R // 2 // PIECE
    away = (nt - 1) * (feat // tile)
    bf = jnp.bfloat16
    hbm = pl.BlockSpec(memory_space=pl.ANY)
    vmem = pl.BlockSpec(memory_space=pltpu.VMEM)
    dma = pltpu.SemaphoreType.DMA
    return pl.pallas_call(
        functools.partial(gather_kernel, n_dp, nt, tile),
        out_shape=(
            jax.ShapeDtypeStruct((n_dp, rank, width), bf),
            jax.ShapeDtypeStruct((rows, feat), bf),
            jax.ShapeDtypeStruct((nt - 1, rows, feat), bf),
        ),
        in_specs=[hbm, vmem, vmem, hbm, hbm],
        out_specs=(hbm, vmem, hbm),
        scratch_shapes=[
            pltpu.VMEM((2, tile, wq.shape[1]), bf),
            pltpu.VMEM((2, tile, wv.shape[1]), bf),
            pltpu.VMEM((away, rows, tile), bf),
            dma((2, 2)),
            dma,
            dma,
            dma,
            dma((2, nz - 1, npiece)),
            dma((2, nz - 1, npiece)),
            dma((2, nz - 1, npiece)),
            dma((2, nz - 1, npiece)),
            dma((2, 2, nz - 1, npiece)),
            dma((2, 2, nz - 1, npiece)),
            dma((away,)),
            dma((away,)),
        ],
        compiler_params=pltpu.CompilerParams(
            collective_id=0, has_side_effects=True, vmem_limit_bytes=40 * 2**20
        ),
    )(mine, cq, cv, wq, wv)


def grads_kernel(
    n_dp, nt, col,
    ranks, ids, tokens, cq, cv,
    aq, av, bq, bv,
    own, from_core, from_z, sq_out, sq_in,
    core_send, core_recv, z_send, z_recv, n_send, n_recv,
):
    nz = n_dp // 2
    me = lax.axis_index("dp")
    t = lax.axis_index("tensor")
    z, c = me // 2, lax.rem(me, 2)
    core = 2 * z + 1 - c
    left, right = me - 2, me + 2
    feat, query, value = tokens.shape[1], cq.shape[1], cv.shape[1]
    npiece = R // PIECE
    f32, bf = jnp.float32, jnp.bfloat16

    greet(z, nz, (left, right, core), t, nt, None)

    def contribute(tenant):
        masked = jnp.where(ids[...] == tenant, ranks[...].astype(f32), 0.0).astype(bf)
        to_a, to_bq, to_bv = masked[: 2 * R], masked[2 * R : 3 * R], masked[3 * R :]

        def over(width, body):
            step = min(col, width)

            def run(i, carry):
                body(pl.multiple_of(i * step, step), step)
                return carry

            lax.fori_loop(0, width // step, run, 0)

        def a_part(at, step):
            got = jnp.dot(to_a, tokens[:, pl.ds(at, step)], preferred_element_type=f32).astype(bf)
            own[tenant, :, pl.ds(at, step)] = got[:R]
            own[tenant, :, pl.ds(pl.multiple_of(feat + at, 128), step)] = got[R:]

        def bq_part(at, step):
            got = jnp.dot(to_bq, cq[:, pl.ds(at, step)], preferred_element_type=f32).astype(bf)
            own[tenant, :, pl.ds(pl.multiple_of(2 * feat + at, 128), step)] = got

        def bv_part(at, step):
            got = jnp.dot(to_bv, cv[:, pl.ds(at, step)], preferred_element_type=f32).astype(bf)
            own[tenant, :, pl.ds(pl.multiple_of(2 * feat + query + at, 128), step)] = got

        over(feat, a_part)
        over(query, bq_part)
        over(value, bv_part)

    def core_copy(zt):
        return remote(
            own.at[2 * zt + 1 - c], from_core.at[zt], core_send.at[zt], core_recv.at[zt],
            {"dp": core},
        )

    def pair_sum(zt):
        core_copy(zt).wait_recv()
        own[2 * zt + c] = (own[2 * zt + c].astype(f32) + from_core[zt].astype(f32)).astype(bf)

    def z_copy(way, zt, p):
        at = pl.ds(p * PIECE, PIECE)
        return remote(
            own.at[2 * zt + c, at], from_z.at[way, zt, at], z_send.at[way, zt, p],
            z_recv.at[way, zt, p], {"dp": right if way == 0 else left},
        )

    def target(way, tau):
        return nz - 1 - (tau - z) if way == 0 else tau - (nz - 1 - z)

    def active(way, tau):
        return tau >= z if way == 0 else tau >= nz - 1 - z

    def pass_on(way, tau, p):
        zt = target(way, tau)

        @pl.when(active(way, tau))
        def _():
            at = pl.ds(p * PIECE, PIECE)

            @pl.when(z > 0 if way == 0 else z < nz - 1)
            def _():
                z_copy(way, zt, p).wait_recv()
                own[2 * zt + c, at] = (
                    own[2 * zt + c, at].astype(f32) + from_z[way, zt, at].astype(f32)
                ).astype(bf)

            z_copy(way, zt, p).start()

    def sent(way, tau, p):
        @pl.when(active(way, tau))
        def _():
            z_copy(way, target(way, tau), p).wait_send()

    order = []
    for j in range((nz + 1) // 2):
        order += [nz - 1 - j] + ([j] if j != nz - 1 - j else [])

    for n, zt in enumerate(order):
        contribute(2 * zt + 1 - c)
        core_copy(zt).start()
        contribute(2 * zt + c)
        if n == 1:
            for earlier in order[:2]:
                pair_sum(earlier)
            for p in range(npiece):
                for way in range(2):
                    @pl.when(z == 0 if way == 0 else z == nz - 1)
                    def _(way=way, p=p):
                        pass_on(way, 0, p)
        elif n > 1:
            pair_sum(zt)

    for tau in range(1, nz - 1):
        for p in range(npiece):
            for way in range(2):
                sent(way, tau - 1, p)
                pass_on(way, tau, p)

    total = jnp.zeros((1, 1), f32)
    places = ((aq, 0, feat), (av, feat, feat), (bq, 2 * feat, query), (bv, 2 * feat + query, value))
    for p in range(npiece):
        at = pl.ds(p * PIECE, PIECE)
        for way in range(2):
            @pl.when(z > 0 if way == 0 else z < nz - 1)
            def _(way=way):
                z_copy(way, z, p).wait_recv()

        have_left, have_right = z > 0, z < nz - 1
        for ref, first, width in places:
            cols = pl.ds(first, width)
            sums = own[me, at, cols].astype(f32)
            ref[at, :] = sums

            @pl.when(have_left)
            def _(ref=ref, cols=cols):
                ref[at, :] += from_z[0, z, at, cols].astype(f32)

            @pl.when(have_right)
            def _(ref=ref, cols=cols):
                ref[at, :] += from_z[1, z, at, cols].astype(f32)

            sums = SCALE * ref[at, :]
            ref[at, :] = sums
            total = total + jnp.sum(sums * sums, axis=(0, 1), keepdims=True)

    sq_out[...] = jnp.broadcast_to(total, sq_out.shape)

    def n_copy(d):
        return remote(
            sq_out, sq_in.at[d], n_send.at[d], n_recv.at[d], {"tensor": lax.rem(t + 1 + d, nt)}
        )

    for d in range(nt - 1):
        n_copy(d).start()
    norm = sq_out[0:1, 0:1]
    for d in range(nt - 1):
        n_copy(d).wait_recv()
        norm = norm + sq_in[d, 0:1, 0:1]
    entries = float(R * (2 * D + QW + KV))
    factor = jnp.minimum(1.0, CLIP_RMS * math.sqrt(entries) / jnp.sqrt(norm + 1e-06))
    for ref, _, _ in places:
        ref[...] = ref[...] * factor

    for d in range(nt - 1):
        n_copy(d).wait_send()
    for zt in range(nz):
        core_copy(zt).wait_send()
    for p in range(npiece):
        for way in range(2):
            sent(way, nz - 2, p)


def grads(ranks, ids, tokens, cq, cv, n_dp, nt):
    feat, query, value = tokens.shape[1], cq.shape[1], cv.shape[1]
    width = 2 * feat + query + value
    nz = n_dp // 2
    npiece = R // PIECE
    bf, f32 = jnp.bfloat16, jnp.float32
    vmem = pl.BlockSpec(memory_space=pltpu.VMEM)
    dma = pltpu.SemaphoreType.DMA
    return pl.pallas_call(
        functools.partial(grads_kernel, n_dp, nt, 1024),
        out_shape=tuple(jax.ShapeDtypeStruct((R, w), f32) for w in (feat, feat, query, value)),
        in_specs=[vmem] * 5,
        out_specs=(vmem,) * 4,
        scratch_shapes=[
            pltpu.VMEM((n_dp, R, width), bf),
            pltpu.VMEM((nz, R, width), bf),
            pltpu.VMEM((2, nz, R, width), bf),
            pltpu.VMEM((8, 128), f32),
            pltpu.VMEM((nt - 1, 8, 128), f32),
            dma((nz,)),
            dma((nz,)),
            dma((2, nz, npiece)),
            dma((2, nz, npiece)),
            dma((nt - 1,)),
            dma((nt - 1,)),
        ],
        compiler_params=pltpu.CompilerParams(
            collective_id=1, has_side_effects=True, vmem_limit_bytes=52 * 2**20
        ),
    )(ranks, ids, tokens, cq, cv)


def on_device(
    n_dp, nt,
    tokens, tenant_ids, cot_query, cot_value, w_query, w_value, a_query, a_value, b_query, b_value
):
    bf, f32 = jnp.bfloat16, jnp.float32
    feat, query = a_query.shape[2], b_query.shape[2]
    rows = tokens.shape[0]
    mine = jnp.concatenate([a_query[0], a_value[0], b_query[0], b_value[0]], axis=1)
    full, frozen, parts = gather(mine, cot_query, cot_value, w_query, w_value, n_dp, nt)
    flat = full.reshape(n_dp * R, full.shape[2])
    flat_aq, flat_av = flat[:, :feat], flat[:, feat : 2 * feat]
    flat_bq, flat_bv = flat[:, 2 * feat : 2 * feat + query], flat[:, 2 * feat + query :]
    mask = tenant_ids[0][:, None] == jnp.arange(n_dp, dtype=jnp.int32)[None, :]

    def pick(part):
        part = part.reshape(rows, n_dp, R)
        return jnp.sum(jnp.where(mask[:, :, None], part, 0.0), axis=1)

    part = jnp.concatenate(
        [
            pick(dot_cols(cot_query, flat_bq)),
            pick(dot_cols(cot_value, flat_bv)),
            pick(dot_cols(tokens, flat_aq)),
            pick(dot_cols(tokens, flat_av)),
        ],
        axis=1,
    ).astype(bf)
    if nt == 2:
        got = lax.ppermute(part, "tensor", [(0, 1), (1, 0)])
        ranks = (part.astype(f32) + got.astype(f32)).astype(bf)
    else:
        ranks = lax.psum(part, "tensor")

    def spread(own):
        return jnp.where(mask[:, :, None], own[:, None, :], 0).reshape(rows, n_dp * R)

    adapter = jnp.dot(spread(ranks[:, :R]), flat_aq, preferred_element_type=f32) + jnp.dot(
        spread(ranks[:, R : 2 * R]), flat_av, preferred_element_type=f32
    )
    total = frozen.astype(f32)
    for d in range(nt - 1):
        total = total + parts[d].astype(f32)
    input_grad = (total + SCALE * adapter).astype(bf)
    outs = grads(ranks.T, tenant_ids, tokens, cot_query, cot_value, n_dp, nt)
    return (input_grad,) + tuple(out[None] for out in outs)


def solution(mesh):
    n_dp, nt = mesh.shape["dp"], mesh.shape["tensor"]
    in_specs = (
        P(("groups", "dp"), "tensor"),
        P(("groups", "dp"), None),
        P(("groups", "dp"), "tensor"),
        P(("groups", "dp"), "tensor"),
        P(None, "tensor"),
        P(None, "tensor"),
        P("dp", None, "tensor"),
        P("dp", None, "tensor"),
        P("dp", None, "tensor"),
        P("dp", None, "tensor"),
    )
    out_specs = (
        P(("groups", "dp"), "tensor"),
        P(("groups", "dp"), None, "tensor"),
        P(("groups", "dp"), None, "tensor"),
        P(("groups", "dp"), None, "tensor"),
        P(("groups", "dp"), None, "tensor"),
    )
    return jax.shard_map(
        functools.partial(on_device, n_dp, nt),
        mesh=mesh, in_specs=in_specs, out_specs=out_specs, check_vma=False,
    )
```

```python
import functools
import math

import jax
import jax.numpy as jnp
from jax import lax
from jax.experimental import pallas as pl
from jax.experimental.pallas import tpu as pltpu
from jax.sharding import PartitionSpec as P

D = 8192
QW = 4096
KV = 1024
R = 64

SCALE = 2.0
CLIP_RMS = 0.5
MESH = pl.DeviceIdType.MESH
PIECE = 16


def dot_cols(left, right):
    return lax.dot_general(
        left, right, (((1,), (1,)), ((), ())), preferred_element_type=jnp.float32
    )


def remote(src, dst, send, recv, where):
    return pltpu.make_async_remote_copy(
        src_ref=src, dst_ref=dst, send_sem=send, recv_sem=recv, device_id=where, device_id_type=MESH
    )


def each(low, high, body):
    def run(i, carry):
        body(i)
        return carry

    lax.fori_loop(low, high, run, 0)


def greet(z, nz, pairs, t, nt, x_partner):
    barrier = pltpu.get_barrier_semaphore()

    def signal(where):
        pl.semaphore_signal(barrier, inc=1, device_id=where, device_id_type=MESH)

    left, right, core = pairs

    @pl.when(z > 0)
    def _():
        signal({"dp": left})

    @pl.when(z < nz - 1)
    def _():
        signal({"dp": right})

    signal({"dp": core})
    if x_partner is not None:
        signal({"groups": x_partner})
    for d in range(nt - 1):
        signal({"tensor": lax.rem(t + 1 + d, nt)})
    always = 1 + (x_partner is not None) + nt - 1
    ends = jnp.where(z > 0, 1, 0) + jnp.where(z < nz - 1, 1, 0)
    pl.semaphore_wait(barrier, always + ends)


def kernel(
    n_dp, nt, tile, col,
    mine, ids, tokens, cq, cv, wq, wv,
    input_grad, aq, av, bq, bv,
    full, own, from_core, from_z, parts, wq_buf, wv_buf, out_buf,
    rk_out, rk_in, rk, spread, sq_out, sq_in,
    w_sem, l_sem, own_send, own_recv, z_send, z_recv, x_send, x_recv, c_send, c_recv,
    p_send, p_recv, r_send, r_recv, k_send, k_recv, s_send, s_recv, n_send, n_recv,
):
    nz = n_dp // 2
    me = lax.axis_index("dp")
    g = lax.axis_index("groups")
    t = lax.axis_index("tensor")
    z, c = me // 2, lax.rem(me, 2)
    other = 1 - g
    core = 2 * z + 1 - c
    left, right = me - 2, me + 2
    half = R // 2
    npiece = half // PIECE
    nsum = R // PIECE
    feat, query, value = tokens.shape[1], cq.shape[1], cv.shape[1]
    f32, bf = jnp.float32, jnp.bfloat16

    def rows(which, p):
        return pl.ds(pl.multiple_of(which * half + p * PIECE, PIECE), PIECE)

    per = feat // tile
    total, away = nt * per, (nt - 1) * per

    def tiles(i, slot):
        peer = lax.rem(t + 1 + i // per, nt)
        at = pl.ds(pl.multiple_of(peer * feat + lax.rem(i, per) * tile, tile), tile)
        return (
            pltpu.make_async_copy(wq.at[at], wq_buf.at[slot], w_sem.at[0, slot]),
            pltpu.make_async_copy(wv.at[at], wv_buf.at[slot], w_sem.at[1, slot]),
        )

    def p_copy(i):
        at = pl.ds(pl.multiple_of(lax.rem(i, per) * tile, tile), tile)
        peer = lax.rem(t + 1 + i // per, nt)
        return remote(
            out_buf.at[i], parts.at[i // per, :, at], p_send.at[i], p_recv.at[i], {"tensor": peer}
        )

    def step(i, carry):
        slot = lax.rem(i, 2)
        for copy in tiles(i, slot):
            copy.wait()

        @pl.when(i + 1 < total)
        def _():
            for copy in tiles(i + 1, 1 - slot):
                copy.start()

        got = dot_cols(cq[...], wq_buf[slot]) + dot_cols(cv[...], wv_buf[slot])
        got = got.astype(bf)

        @pl.when(i < away)
        def _():
            out_buf[i] = got
            p_copy(i).start()

        @pl.when(i >= away)
        def _():
            at = pl.ds(pl.multiple_of(lax.rem(i, per) * tile, tile), tile)
            input_grad[:, at] = got

        return carry

    def frozen(part):
        lax.fori_loop(part * total // nz, (part + 1) * total // nz, step, 0)

    for copy in tiles(0, 0):
        copy.start()

    greet(z, nz, (left, right, core), t, nt, other)

    def dest(way, j):
        return z + (1 - 2 * way) * j

    def goes(way, j):
        return jnp.logical_and(dest(way, j) >= 0, dest(way, j) <= nz - 1)

    def far(way, k):
        return z - (1 - 2 * way) * k

    def there(way, k):
        return jnp.logical_and(far(way, k) >= 0, far(way, k) <= nz - 1)

    def ahead(way):
        return {"dp": me + 2 * (1 - 2 * way)}

    def z_copy(way, k, p):
        at = full.at[2 * far(way, k) + c, rows(g, p)]
        return remote(at, at, z_send.at[way, k, p], z_recv.at[way, k, p], ahead(way))

    def z_arrival(way, k, p):
        at = full.at[2 * far(way, k + 1) + c, rows(g, p)]
        return remote(at, at, z_send.at[way, k, p], z_recv.at[way, k, p], ahead(way))

    def x_copy(way, k, p, arriving):
        at = full.at[2 * far(way, k + 1) + c, rows(other if arriving else g, p)]
        return remote(at, at, x_send.at[way, k, p], x_recv.at[way, k, p], {"groups": other})

    def c_copy(which, way, k, p, arriving):
        slot = 2 * far(way, k + 1) + (1 - c if arriving else c)
        at = full.at[slot, rows(g if which == 0 else other, p)]
        return remote(
            at, at, c_send.at[which, way, k, p], c_recv.at[which, way, k, p], {"dp": core}
        )

    def sends(way, k):
        return jnp.logical_and(there(way, k), goes(way, 1))

    def both(cond, body):
        def one(way):
            @pl.when(cond(way))
            def _():
                body(way)

        each(0, 2, one)

    def pieces(cond, body):
        each(0, npiece, lambda p: both(cond, lambda way: body(way, p)))

    local = pltpu.make_async_copy(mine, full.at[me], l_sem)
    local.start()
    local.wait()
    pieces(lambda way: sends(way, 0), lambda way, p: z_copy(way, 0, p).start())
    own_out = remote(mine, full.at[me], own_send, own_recv, {"dp": core})
    own_out.start()
    own_in = remote(mine, full.at[core], own_send, own_recv, {"dp": core})

    def arrive(k):
        def here(way):
            return there(way, k + 1)

        def from_line(way, p):
            z_arrival(way, k, p).wait_recv()

            @pl.when(sends(way, k + 1))
            def _():
                z_copy(way, k + 1, p).start()

            x_copy(way, k, p, False).start()
            c_copy(0, way, k, p, False).start()

        def from_x(way, p):
            x_copy(way, k, p, True).wait_recv()
            c_copy(1, way, k, p, False).start()

        def from_pair(way, p):
            for which in range(2):
                c_copy(which, way, k, p, True).wait_recv()

        pieces(here, from_line)
        pieces(here, from_x)
        pieces(here, from_pair)

    def k_copy(zt, d):
        return remote(
            rk_out.at[zt], rk_in.at[d, zt], k_send.at[zt, d], k_recv.at[zt, d],
            {"tensor": lax.rem(t + 1 + d, nt)},
        )

    def partial(zt):
        def product(first, width, right_ref, spans):
            wide = min(512, width)

            def run(i, acc):
                at = i * wide
                stack = [
                    full[2 * zt + s, :, pl.ds(pl.multiple_of(first + j * width + at, 128), wide)]
                    for s in range(2)
                    for j in range(spans)
                ]
                cols = pl.ds(pl.multiple_of(at, 128), wide)
                return acc + dot_cols(jnp.concatenate(stack, axis=0), right_ref[:, cols])

            zero = jnp.zeros((2 * spans * R, tokens.shape[0]), f32)
            return lax.fori_loop(0, width // wide, run, zero)

        h = product(0, feat, tokens, 2)
        gq = product(2 * feat, query, cq, 1)
        gv = product(2 * feat + query, value, cv, 1)
        two = []
        for s in range(2):
            rank = jnp.concatenate(
                [gq[s * R : (s + 1) * R], gv[s * R : (s + 1) * R], h[2 * s * R : 2 * (s + 1) * R]],
                axis=0,
            )
            two.append(jnp.where(ids[...] == 2 * zt + s, rank, 0.0))
        rk_out[zt] = (two[0] + two[1]).astype(bf)
        for d in range(nt - 1):
            k_copy(zt, d).start()

    def core_copy(zt):
        return remote(
            own.at[2 * zt + 1 - c], from_core.at[zt], s_send.at[zt], s_recv.at[zt], {"dp": core}
        )

    def contribute(zt):
        summed = rk_out[zt].astype(f32)
        for d in range(nt - 1):
            k_copy(zt, d).wait_recv()
            summed = summed + rk_in[d, zt].astype(f32)
        rk[...] = summed.astype(bf)
        masked = []
        for s in range(2):
            keep = jnp.where(ids[...] == 2 * zt + s, rk[...].astype(f32), 0.0).astype(bf)
            masked.append(keep)
            at = pl.ds(pl.multiple_of((2 * zt + s) * R, R), R)
            spread[0, at, :] = keep[:R]
            spread[1, at, :] = keep[R : 2 * R]

        def over(first, width, right_ref, low, spans):
            wide = min(col, width)
            lhs = jnp.concatenate([m[low * R : (low + spans) * R] for m in masked], axis=0)

            def run(i, carry):
                at = pl.multiple_of(i * wide, 128)
                got = jnp.dot(lhs, right_ref[:, pl.ds(at, wide)], preferred_element_type=f32)
                got = got.astype(bf)
                for s in range(2):
                    for j in range(spans):
                        cols = pl.ds(pl.multiple_of(first + j * width + at, 128), wide)
                        low_row = (s * spans + j) * R
                        own[2 * zt + s, :, cols] = got[low_row : low_row + R]
                return carry

            lax.fori_loop(0, width // wide, run, 0)

        over(0, feat, tokens, 0, 2)
        over(2 * feat, query, cq, 2, 1)
        over(2 * feat + query, value, cv, 3, 1)
        core_copy(zt).start()

    def pair_sum(zt):
        core_copy(zt).wait_recv()
        mine_at = 2 * zt + c

        def add(p):
            at = pl.ds(pl.multiple_of(p * PIECE, PIECE), PIECE)
            own[mine_at, at] = (
                own[mine_at, at].astype(f32) + from_core[zt, at].astype(f32)
            ).astype(bf)

        each(0, nsum, add)

    def slot_of(way, zt, last):
        return zt + jnp.where(last, way * (nz - zt), 0)

    def r_copy(way, j, p):
        zt = dest(way, j)
        at = pl.ds(pl.multiple_of(p * PIECE, PIECE), PIECE)
        return remote(
            own.at[2 * zt + c, at], from_z.at[slot_of(way, zt, j == 1), at],
            r_send.at[way, zt, p], r_recv.at[way, zt, p], ahead(way),
        )

    def r_arrival(way, j, p):
        zt = dest(way, j)
        at = pl.ds(pl.multiple_of(p * PIECE, PIECE), PIECE)
        ref = from_z.at[slot_of(way, zt, j == 0), at]
        return remote(ref, ref, r_send.at[way, zt, p], r_recv.at[way, zt, p], ahead(way))

    def start_sum(way, j, p):
        before = (j - 1) * nsum + p - 2

        @pl.when(before >= 0)
        def _():
            r_copy(way, before // nsum + 1, lax.rem(before, nsum)).wait_send()

        r_copy(way, j, p).start()

    def first_of(way):
        return z == way * (nz - 1)

    frozen(0)
    own_in.wait_recv()
    partial(z)

    def distance(k):
        def on(way):
            return goes(way, k)

        def gradients(way):
            contribute(dest(way, k))

        def send_first(way):
            each(0, nsum, lambda p: start_sum(way, k, p))

        arrive(k - 1)
        both(on, lambda way: partial(dest(way, k)))
        both(on, gradients)
        both(on, lambda way: pair_sum(dest(way, k)))
        both(lambda way: jnp.logical_and(on(way), first_of(way)), send_first)
        frozen(k)

    each(1, nz, distance)
    contribute(z)
    pair_sum(z)

    def finish(i, carry):
        p_copy(i).wait_recv()
        return carry

    lax.fori_loop(0, away, finish, 0)

    def add_adapters(i, carry):
        wide = min(512, feat)
        at = pl.multiple_of(i * wide, 128)
        rows_in = (((0,), (0,)), ((), ()))
        sums = input_grad[:, pl.ds(at, wide)].astype(f32)
        for d in range(nt - 1):
            sums = sums + parts[d, :, pl.ds(at, wide)].astype(f32)
        for j in range(2):
            cols = pl.ds(pl.multiple_of(j * feat + at, 128), wide)
            maps = full[:, :, cols].reshape(n_dp * R, wide)
            sums = sums + SCALE * lax.dot_general(
                spread[j], maps, rows_in, preferred_element_type=f32
            )
        input_grad[:, pl.ds(at, wide)] = sums.astype(bf)
        return carry

    lax.fori_loop(0, feat // min(512, feat), add_adapters, 0)

    def pass_on(time):
        def left_to_go(way):
            return time - 2 * (z + way * (nz - 1 - 2 * z))

        def add(way, p):
            j = left_to_go(way)
            r_arrival(way, j, p).wait_recv()
            at = pl.ds(pl.multiple_of(p * PIECE, PIECE), PIECE)
            zt = dest(way, j)
            own[2 * zt + c, at] = (
                own[2 * zt + c, at].astype(f32) + from_z[zt, at].astype(f32)
            ).astype(bf)
            start_sum(way, j, p)

        def inner(way):
            j = left_to_go(way)
            valid = jnp.logical_and(j >= 1, goes(way, j))
            return jnp.logical_and(valid, jnp.logical_not(first_of(way)))

        each(0, nsum, lambda p: both(inner, lambda way: add(way, p)))

    each(1, 2 * nz - 2, pass_on)

    places = ((aq, 0, feat), (av, feat, feat), (bq, 2 * feat, query), (bv, 2 * feat + query, value))

    def collect(p, norm):
        at = pl.ds(pl.multiple_of(p * PIECE, PIECE), PIECE)
        both(lambda way: there(way, 1), lambda way: r_arrival(way, 0, p).wait_recv())
        for ref, first, width in places:
            ref[at, :] = own[me, at, pl.ds(first, width)].astype(f32)

        def add(way):
            for ref, first, width in places:
                cols = pl.ds(first, width)
                ref[at, :] += from_z[slot_of(way, z, True), at, cols].astype(f32)

        both(lambda way: there(way, 1), add)
        for ref, _, _ in places:
            sums = SCALE * ref[at, :]
            ref[at, :] = sums
            norm = norm + jnp.sum(sums * sums, axis=(0, 1), keepdims=True)
        return norm

    norm = lax.fori_loop(0, nsum, collect, jnp.zeros((1, 1), f32))
    sq_out[...] = jnp.broadcast_to(norm, sq_out.shape)

    def n_copy(d):
        return remote(
            sq_out, sq_in.at[d], n_send.at[d], n_recv.at[d], {"tensor": lax.rem(t + 1 + d, nt)}
        )

    for d in range(nt - 1):
        n_copy(d).start()
    norm = sq_out[0:1, 0:1]
    for d in range(nt - 1):
        n_copy(d).wait_recv()
        norm = norm + sq_in[d, 0:1, 0:1]
    entries = float(R * (2 * D + QW + KV))
    factor = jnp.minimum(1.0, CLIP_RMS * math.sqrt(entries) / jnp.sqrt(norm + 1e-06))
    for ref, _, _ in places:
        ref[...] = ref[...] * factor

    for d in range(nt - 1):
        n_copy(d).wait_send()
    def pair_left(zt):
        core_copy(zt).wait_send()
        for d in range(nt - 1):
            k_copy(zt, d).wait_send()

    each(0, nz, pair_left)
    own_out.wait_send()

    def gather_left(k):
        def shared(way, p):
            for which in range(2):
                c_copy(which, way, k, p, False).wait_send()
            x_copy(way, k, p, False).wait_send()

        pieces(lambda way: there(way, k + 1), shared)
        pieces(lambda way: sends(way, k), lambda way, p: z_copy(way, k, p).wait_send())

    each(0, nz - 1, gather_left)

    def sums_left(j):
        def last(way):
            return jnp.logical_and(goes(way, j), jnp.logical_not(goes(way, j + 1)))

        each(nsum - 2, nsum, lambda p: both(last, lambda way: r_copy(way, j, p).wait_send()))

    each(1, nz, sums_left)

    def left_all(i, carry):
        p_copy(i).wait_send()
        return carry

    lax.fori_loop(0, away, left_all, 0)


def on_device(
    n_dp, nt,
    tokens, tenant_ids, cot_query, cot_value, w_query, w_value, a_query, a_value, b_query, b_value
):
    bf, f32 = jnp.bfloat16, jnp.float32
    feat, query, value = tokens.shape[1], cot_query.shape[1], cot_value.shape[1]
    rows = tokens.shape[0]
    mine = jnp.concatenate([a_query[0], a_value[0], b_query[0], b_value[0]], axis=1)
    width = mine.shape[1]
    tile = min(256, feat)
    nz = n_dp // 2
    npiece, nsum = R // 2 // PIECE, R // PIECE
    away = (nt - 1) * (feat // tile)
    hbm = pl.BlockSpec(memory_space=pl.ANY)
    vmem = pl.BlockSpec(memory_space=pltpu.VMEM)
    dma = pltpu.SemaphoreType.DMA
    outs = pl.pallas_call(
        functools.partial(kernel, n_dp, nt, tile, 1024),
        out_shape=(jax.ShapeDtypeStruct((rows, feat), bf),)
        + tuple(jax.ShapeDtypeStruct((R, w), f32) for w in (feat, feat, query, value)),
        in_specs=[hbm, vmem, vmem, vmem, vmem, hbm, hbm],
        out_specs=(vmem,) * 5,
        scratch_shapes=[
            pltpu.VMEM((n_dp, R, width), bf),
            pltpu.VMEM((n_dp, R, width), bf),
            pltpu.VMEM((nz, R, width), bf),
            pltpu.VMEM((nz + 1, R, width), bf),
            pltpu.VMEM((nt - 1, rows, feat), bf),
            pltpu.VMEM((2, tile, query), bf),
            pltpu.VMEM((2, tile, value), bf),
            pltpu.VMEM((away, rows, tile), bf),
            pltpu.VMEM((nz, 4 * R, rows), bf),
            pltpu.VMEM((nt - 1, nz, 4 * R, rows), bf),
            pltpu.VMEM((4 * R, rows), bf),
            pltpu.VMEM((2, n_dp * R, rows), bf),
            pltpu.VMEM((8, 128), f32),
            pltpu.VMEM((nt - 1, 8, 128), f32),
            dma((2, 2)),
            dma,
            dma,
            dma,
            dma((2, nz - 1, npiece)),
            dma((2, nz - 1, npiece)),
            dma((2, nz - 1, npiece)),
            dma((2, nz - 1, npiece)),
            dma((2, 2, nz - 1, npiece)),
            dma((2, 2, nz - 1, npiece)),
            dma((away,)),
            dma((away,)),
            dma((2, nz, nsum)),
            dma((2, nz, nsum)),
            dma((nz, nt - 1)),
            dma((nz, nt - 1)),
            dma((nz,)),
            dma((nz,)),
            dma((nt - 1,)),
            dma((nt - 1,)),
        ],
        compiler_params=pltpu.CompilerParams(
            collective_id=0, has_side_effects=True, vmem_limit_bytes=57 * 2**20
        ),
    )(mine, tenant_ids, tokens, cot_query, cot_value, w_query, w_value)
    return (outs[0],) + tuple(out[None] for out in outs[1:])


def solution(mesh):
    n_dp, nt = mesh.shape["dp"], mesh.shape["tensor"]
    in_specs = (
        P(("groups", "dp"), "tensor"),
        P(("groups", "dp"), None),
        P(("groups", "dp"), "tensor"),
        P(("groups", "dp"), "tensor"),
        P(None, "tensor"),
        P(None, "tensor"),
        P("dp", None, "tensor"),
        P("dp", None, "tensor"),
        P("dp", None, "tensor"),
        P("dp", None, "tensor"),
    )
    out_specs = (
        P(("groups", "dp"), "tensor"),
        P(("groups", "dp"), None, "tensor"),
        P(("groups", "dp"), None, "tensor"),
        P(("groups", "dp"), None, "tensor"),
        P(("groups", "dp"), None, "tensor"),
    )
    return jax.shard_map(
        functools.partial(on_device, n_dp, nt),
        mesh=mesh, in_specs=in_specs, out_specs=out_specs, check_vma=False,
    )
```

```python
import functools
import math

import jax
import jax.numpy as jnp
from jax import lax
from jax.experimental import pallas as pl
from jax.experimental.pallas import tpu as pltpu
from jax.sharding import PartitionSpec as P

D = 8192
QW = 4096
KV = 1024
R = 64

SCALE = 2.0
CLIP_RMS = 0.5
MESH = pl.DeviceIdType.MESH
PIECE = 16


def dot_cols(left, right):
    return lax.dot_general(
        left, right, (((1,), (1,)), ((), ())), preferred_element_type=jnp.float32
    )


def remote(src, dst, send, recv, where):
    return pltpu.make_async_remote_copy(
        src_ref=src, dst_ref=dst, send_sem=send, recv_sem=recv, device_id=where, device_id_type=MESH
    )


def greet(z, nz, pairs, t, nt, x_partner):
    barrier = pltpu.get_barrier_semaphore()

    def signal(where):
        pl.semaphore_signal(barrier, inc=1, device_id=where, device_id_type=MESH)

    left, right, core = pairs

    @pl.when(z > 0)
    def _():
        signal({"dp": left})

    @pl.when(z < nz - 1)
    def _():
        signal({"dp": right})

    signal({"dp": core})
    if x_partner is not None:
        signal({"groups": x_partner})
    for d in range(nt - 1):
        signal({"tensor": lax.rem(t + 1 + d, nt)})
    always = 1 + (x_partner is not None) + nt - 1
    ends = jnp.where(z > 0, 1, 0) + jnp.where(z < nz - 1, 1, 0)
    pl.semaphore_wait(barrier, always + ends)


def gather_kernel(
    n_dp, nt, tile,
    mine, cq, cv, wq, wv,
    full, frozen, parts,
    wq_buf, wv_buf, out_buf,
    w_sem, l_sem, own_send, own_recv, z_send, z_recv, x_send, x_recv, c_send, c_recv,
    p_send, p_recv,
):
    nz = n_dp // 2
    me = lax.axis_index("dp")
    g = lax.axis_index("groups")
    t = lax.axis_index("tensor")
    z, c = me // 2, lax.rem(me, 2)
    other = 1 - g
    core = 2 * z + 1 - c
    left, right = me - 2, me + 2
    half = R // 2
    npiece = half // PIECE

    def rows(which, p):
        return pl.ds(pl.multiple_of(which * half + p * PIECE, PIECE), PIECE)

    def tiles(i, slot):
        per = frozen.shape[1] // tile
        peer = lax.rem(t + 1 + i // per, nt)
        at = pl.ds(pl.multiple_of(peer * frozen.shape[1] + lax.rem(i, per) * tile, tile), tile)
        return (
            pltpu.make_async_copy(wq.at[at], wq_buf.at[slot], w_sem.at[0, slot]),
            pltpu.make_async_copy(wv.at[at], wv_buf.at[slot], w_sem.at[1, slot]),
        )

    for copy in tiles(0, 0):
        copy.start()

    greet(z, nz, (left, right, core), t, nt, other)

    def z_copy(way, k, p, source):
        slot = 2 * (z - k if way == 0 else z + k) + c
        at = rows(g, p)
        src = mine.at[at] if source else full.at[slot, at]
        return remote(
            src, full.at[slot, at], z_send.at[way, k, p], z_recv.at[way, k, p],
            {"dp": right if way == 0 else left},
        )

    def z_arrival(way, k, p):
        slot = 2 * (z - k - 1 if way == 0 else z + k + 1) + c
        at = full.at[slot, rows(g, p)]
        return remote(
            at, at, z_send.at[way, k, p], z_recv.at[way, k, p],
            {"dp": right if way == 0 else left},
        )

    def x_copy(way, k, p, arriving):
        slot = 2 * (z - k - 1 if way == 0 else z + k + 1) + c
        at = full.at[slot, rows(other if arriving else g, p)]
        return remote(at, at, x_send.at[way, k, p], x_recv.at[way, k, p], {"groups": other})

    def c_copy(which, way, k, p, arriving):
        slot = 2 * (z - k - 1 if way == 0 else z + k + 1) + (1 - c if arriving else c)
        at = full.at[slot, rows(g if which == 0 else other, p)]
        return remote(
            at, at, c_send.at[which, way, k, p], c_recv.at[which, way, k, p], {"dp": core}
        )

    def sends(way, k):
        if way == 0:
            return jnp.logical_and(z - k >= 0, z < nz - 1)
        return jnp.logical_and(z + k <= nz - 1, z > 0)

    def gets(way, k):
        return z - k - 1 >= 0 if way == 0 else z + k + 1 <= nz - 1

    for p in range(npiece):
        for way in range(2):
            @pl.when(sends(way, 0))
            def _(way=way, p=p):
                z_copy(way, 0, p, True).start()

    local = pltpu.make_async_copy(mine, full.at[me], l_sem)
    local.start()
    own = remote(mine, full.at[me], own_send, own_recv, {"dp": core})
    own.start()
    own_in = remote(mine, full.at[core], own_send, own_recv, {"dp": core})

    per = frozen.shape[1] // tile
    total, away = nt * per, (nt - 1) * per

    def p_copy(i):
        at = pl.ds(pl.multiple_of(lax.rem(i, per) * tile, tile), tile)
        peer = lax.rem(t + 1 + i // per, nt)
        return remote(
            out_buf.at[i], parts.at[i // per, :, at], p_send.at[i], p_recv.at[i], {"tensor": peer}
        )

    def step(i, carry):
        slot = lax.rem(i, 2)
        for copy in tiles(i, slot):
            copy.wait()

        @pl.when(i + 1 < total)
        def _():
            for copy in tiles(i + 1, 1 - slot):
                copy.start()

        value = dot_cols(cq[...], wq_buf[slot]) + dot_cols(cv[...], wv_buf[slot])
        value = value.astype(jnp.bfloat16)

        @pl.when(i < away)
        def _():
            out_buf[i] = value
            p_copy(i).start()

        @pl.when(i >= away)
        def _():
            at = pl.ds(pl.multiple_of(lax.rem(i, per) * tile, tile), tile)
            frozen[:, at] = value

        return carry

    lax.fori_loop(0, total // 2, step, 0)

    def from_x(k):
        for p in range(npiece):
            for way in range(2):
                @pl.when(gets(way, k))
                def _(way=way, p=p):
                    x_copy(way, k, p, True).wait_recv()
                    c_copy(1, way, k, p, False).start()

    cuts = [total // 2 + (total - total // 2) * n // npiece for n in range(npiece + 1)]
    for k in range(nz - 1):
        for p in range(npiece):
            for way in range(2):
                @pl.when(gets(way, k))
                def _(way=way, p=p, k=k):
                    z_arrival(way, k, p).wait_recv()
                    if k + 1 < nz - 1:
                        @pl.when(sends(way, k + 1))
                        def _():
                            z_copy(way, k + 1, p, False).start()
                    x_copy(way, k, p, False).start()
                    c_copy(0, way, k, p, False).start()
            if k == 0:
                lax.fori_loop(cuts[p], cuts[p + 1], step, 0)
        if k > 0:
            from_x(k - 1)
    from_x(nz - 2)

    own_in.wait_recv()
    for k in range(nz - 1):
        for p in range(npiece):
            for way in range(2):
                @pl.when(gets(way, k))
                def _(way=way, p=p, k=k):
                    for which in range(2):
                        c_copy(which, way, k, p, True).wait_recv()
                        c_copy(which, way, k, p, False).wait_send()
                    x_copy(way, k, p, False).wait_send()

                @pl.when(sends(way, k))
                def _(way=way, p=p, k=k):
                    z_copy(way, k, p, k == 0).wait_send()
    own.wait_send()
    local.wait()

    def finish(i, carry):
        p_copy(i).wait_recv()
        p_copy(i).wait_send()
        return carry

    lax.fori_loop(0, away, finish, 0)


def gather(mine, cq, cv, wq, wv, n_dp, nt):
    rank, width = mine.shape
    rows = cq.shape[0]
    feat = wq.shape[0] // nt
    tile = min(512, feat)
    nz = n_dp // 2
    npiece = R // 2 // PIECE
    away = (nt - 1) * (feat // tile)
    bf = jnp.bfloat16
    hbm = pl.BlockSpec(memory_space=pl.ANY)
    vmem = pl.BlockSpec(memory_space=pltpu.VMEM)
    dma = pltpu.SemaphoreType.DMA
    return pl.pallas_call(
        functools.partial(gather_kernel, n_dp, nt, tile),
        out_shape=(
            jax.ShapeDtypeStruct((n_dp, rank, width), bf),
            jax.ShapeDtypeStruct((rows, feat), bf),
            jax.ShapeDtypeStruct((nt - 1, rows, feat), bf),
        ),
        in_specs=[hbm, vmem, vmem, hbm, hbm],
        out_specs=(hbm, vmem, hbm),
        scratch_shapes=[
            pltpu.VMEM((2, tile, wq.shape[1]), bf),
            pltpu.VMEM((2, tile, wv.shape[1]), bf),
            pltpu.VMEM((away, rows, tile), bf),
            dma((2, 2)),
            dma,
            dma,
            dma,
            dma((2, nz - 1, npiece)),
            dma((2, nz - 1, npiece)),
            dma((2, nz - 1, npiece)),
            dma((2, nz - 1, npiece)),
            dma((2, 2, nz - 1, npiece)),
            dma((2, 2, nz - 1, npiece)),
            dma((away,)),
            dma((away,)),
        ],
        compiler_params=pltpu.CompilerParams(
            collective_id=0, has_side_effects=True, vmem_limit_bytes=40 * 2**20
        ),
    )(mine, cq, cv, wq, wv)


def grads_kernel(
    n_dp, nt, col,
    ranks, ids, tokens, cq, cv,
    aq, av, bq, bv,
    own, from_core, from_z, sq_out, sq_in,
    core_send, core_recv, z_send, z_recv, n_send, n_recv,
):
    nz = n_dp // 2
    me = lax.axis_index("dp")
    t = lax.axis_index("tensor")
    z, c = me // 2, lax.rem(me, 2)
    core = 2 * z + 1 - c
    left, right = me - 2, me + 2
    feat, query, value = tokens.shape[1], cq.shape[1], cv.shape[1]
    npiece = R // PIECE
    f32, bf = jnp.float32, jnp.bfloat16

    greet(z, nz, (left, right, core), t, nt, None)

    def contribute(tenant):
        masked = jnp.where(ids[...] == tenant, ranks[...].astype(f32), 0.0).astype(bf)
        to_a, to_bq, to_bv = masked[: 2 * R], masked[2 * R : 3 * R], masked[3 * R :]

        def over(width, body):
            step = min(col, width)

            def run(i, carry):
                body(pl.multiple_of(i * step, step), step)
                return carry

            lax.fori_loop(0, width // step, run, 0)

        def a_part(at, step):
            got = jnp.dot(to_a, tokens[:, pl.ds(at, step)], preferred_element_type=f32).astype(bf)
            own[tenant, :, pl.ds(at, step)] = got[:R]
            own[tenant, :, pl.ds(pl.multiple_of(feat + at, 128), step)] = got[R:]

        def bq_part(at, step):
            got = jnp.dot(to_bq, cq[:, pl.ds(at, step)], preferred_element_type=f32).astype(bf)
            own[tenant, :, pl.ds(pl.multiple_of(2 * feat + at, 128), step)] = got

        def bv_part(at, step):
            got = jnp.dot(to_bv, cv[:, pl.ds(at, step)], preferred_element_type=f32).astype(bf)
            own[tenant, :, pl.ds(pl.multiple_of(2 * feat + query + at, 128), step)] = got

        over(feat, a_part)
        over(query, bq_part)
        over(value, bv_part)

    def core_copy(zt):
        return remote(
            own.at[2 * zt + 1 - c], from_core.at[zt], core_send.at[zt], core_recv.at[zt],
            {"dp": core},
        )

    def pair_sum(zt):
        core_copy(zt).wait_recv()
        own[2 * zt + c] = (own[2 * zt + c].astype(f32) + from_core[zt].astype(f32)).astype(bf)

    def z_copy(way, zt, p):
        at = pl.ds(p * PIECE, PIECE)
        return remote(
            own.at[2 * zt + c, at], from_z.at[way, zt, at], z_send.at[way, zt, p],
            z_recv.at[way, zt, p], {"dp": right if way == 0 else left},
        )

    def target(way, tau):
        return nz - 1 - (tau - z) if way == 0 else tau - (nz - 1 - z)

    def active(way, tau):
        return tau >= z if way == 0 else tau >= nz - 1 - z

    def pass_on(way, tau, p):
        zt = target(way, tau)

        @pl.when(active(way, tau))
        def _():
            at = pl.ds(p * PIECE, PIECE)

            @pl.when(z > 0 if way == 0 else z < nz - 1)
            def _():
                z_copy(way, zt, p).wait_recv()
                own[2 * zt + c, at] = (
                    own[2 * zt + c, at].astype(f32) + from_z[way, zt, at].astype(f32)
                ).astype(bf)

            z_copy(way, zt, p).start()

    def sent(way, tau, p):
        @pl.when(active(way, tau))
        def _():
            z_copy(way, target(way, tau), p).wait_send()

    order = []
    for j in range((nz + 1) // 2):
        order += [nz - 1 - j] + ([j] if j != nz - 1 - j else [])

    for n, zt in enumerate(order):
        contribute(2 * zt + 1 - c)
        core_copy(zt).start()
        contribute(2 * zt + c)
        pair_sum(zt)
        if n < 2:
            @pl.when(z == 0 if n == 0 else z == nz - 1)
            def _(n=n):
                for p in range(npiece):
                    pass_on(n, 0, p)

    for tau in range(1, nz - 1):
        for p in range(npiece):
            for way in range(2):
                sent(way, tau - 1, p)
                pass_on(way, tau, p)

    total = jnp.zeros((1, 1), f32)
    places = ((aq, 0, feat), (av, feat, feat), (bq, 2 * feat, query), (bv, 2 * feat + query, value))
    for p in range(npiece):
        at = pl.ds(p * PIECE, PIECE)
        for way in range(2):
            @pl.when(z > 0 if way == 0 else z < nz - 1)
            def _(way=way):
                z_copy(way, z, p).wait_recv()

        have_left, have_right = z > 0, z < nz - 1
        for ref, first, width in places:
            cols = pl.ds(first, width)
            sums = own[me, at, cols].astype(f32)
            ref[at, :] = sums

            @pl.when(have_left)
            def _(ref=ref, cols=cols):
                ref[at, :] += from_z[0, z, at, cols].astype(f32)

            @pl.when(have_right)
            def _(ref=ref, cols=cols):
                ref[at, :] += from_z[1, z, at, cols].astype(f32)

            sums = SCALE * ref[at, :]
            ref[at, :] = sums
            total = total + jnp.sum(sums * sums, axis=(0, 1), keepdims=True)

    sq_out[...] = jnp.broadcast_to(total, sq_out.shape)

    def n_copy(d):
        return remote(
            sq_out, sq_in.at[d], n_send.at[d], n_recv.at[d], {"tensor": lax.rem(t + 1 + d, nt)}
        )

    for d in range(nt - 1):
        n_copy(d).start()
    norm = sq_out[0:1, 0:1]
    for d in range(nt - 1):
        n_copy(d).wait_recv()
        norm = norm + sq_in[d, 0:1, 0:1]
    entries = float(R * (2 * D + QW + KV))
    factor = jnp.minimum(1.0, CLIP_RMS * math.sqrt(entries) / jnp.sqrt(norm + 1e-06))
    for ref, _, _ in places:
        ref[...] = ref[...] * factor

    for d in range(nt - 1):
        n_copy(d).wait_send()
    for zt in range(nz):
        core_copy(zt).wait_send()
    for p in range(npiece):
        for way in range(2):
            sent(way, nz - 2, p)


def grads(ranks, ids, tokens, cq, cv, n_dp, nt):
    feat, query, value = tokens.shape[1], cq.shape[1], cv.shape[1]
    width = 2 * feat + query + value
    nz = n_dp // 2
    npiece = R // PIECE
    bf, f32 = jnp.bfloat16, jnp.float32
    vmem = pl.BlockSpec(memory_space=pltpu.VMEM)
    dma = pltpu.SemaphoreType.DMA
    return pl.pallas_call(
        functools.partial(grads_kernel, n_dp, nt, 1024),
        out_shape=tuple(jax.ShapeDtypeStruct((R, w), f32) for w in (feat, feat, query, value)),
        in_specs=[vmem] * 5,
        out_specs=(vmem,) * 4,
        scratch_shapes=[
            pltpu.VMEM((n_dp, R, width), bf),
            pltpu.VMEM((nz, R, width), bf),
            pltpu.VMEM((2, nz, R, width), bf),
            pltpu.VMEM((8, 128), f32),
            pltpu.VMEM((nt - 1, 8, 128), f32),
            dma((nz,)),
            dma((nz,)),
            dma((2, nz, npiece)),
            dma((2, nz, npiece)),
            dma((nt - 1,)),
            dma((nt - 1,)),
        ],
        compiler_params=pltpu.CompilerParams(
            collective_id=1, has_side_effects=True, vmem_limit_bytes=52 * 2**20
        ),
    )(ranks, ids, tokens, cq, cv)


def on_device(
    n_dp, nt,
    tokens, tenant_ids, cot_query, cot_value, w_query, w_value, a_query, a_value, b_query, b_value
):
    bf, f32 = jnp.bfloat16, jnp.float32
    feat, query = a_query.shape[2], b_query.shape[2]
    rows = tokens.shape[0]
    mine = jnp.concatenate([a_query[0], a_value[0], b_query[0], b_value[0]], axis=1)
    full, frozen, parts = gather(mine, cot_query, cot_value, w_query, w_value, n_dp, nt)
    flat = full.reshape(n_dp * R, full.shape[2])
    flat_aq, flat_av = flat[:, :feat], flat[:, feat : 2 * feat]
    flat_bq, flat_bv = flat[:, 2 * feat : 2 * feat + query], flat[:, 2 * feat + query :]
    mask = tenant_ids[0][:, None] == jnp.arange(n_dp, dtype=jnp.int32)[None, :]

    def pick(part):
        part = part.reshape(rows, n_dp, R)
        return jnp.sum(jnp.where(mask[:, :, None], part, 0.0), axis=1)

    part = jnp.concatenate(
        [
            pick(dot_cols(cot_query, flat_bq)),
            pick(dot_cols(cot_value, flat_bv)),
            pick(dot_cols(tokens, flat_aq)),
            pick(dot_cols(tokens, flat_av)),
        ],
        axis=1,
    ).astype(bf)
    if nt == 2:
        got = lax.ppermute(part, "tensor", [(0, 1), (1, 0)])
        ranks = (part.astype(f32) + got.astype(f32)).astype(bf)
    else:
        ranks = lax.psum(part, "tensor")

    def spread(own):
        return jnp.where(mask[:, :, None], own[:, None, :], 0).reshape(rows, n_dp * R)

    adapter = jnp.dot(spread(ranks[:, :R]), flat_aq, preferred_element_type=f32) + jnp.dot(
        spread(ranks[:, R : 2 * R]), flat_av, preferred_element_type=f32
    )
    total = frozen.astype(f32)
    for d in range(nt - 1):
        total = total + parts[d].astype(f32)
    input_grad = (total + SCALE * adapter).astype(bf)
    outs = grads(ranks.T, tenant_ids, tokens, cot_query, cot_value, n_dp, nt)
    return (input_grad,) + tuple(out[None] for out in outs)


def solution(mesh):
    n_dp, nt = mesh.shape["dp"], mesh.shape["tensor"]
    in_specs = (
        P(("groups", "dp"), "tensor"),
        P(("groups", "dp"), None),
        P(("groups", "dp"), "tensor"),
        P(("groups", "dp"), "tensor"),
        P(None, "tensor"),
        P(None, "tensor"),
        P("dp", None, "tensor"),
        P("dp", None, "tensor"),
        P("dp", None, "tensor"),
        P("dp", None, "tensor"),
    )
    out_specs = (
        P(("groups", "dp"), "tensor"),
        P(("groups", "dp"), None, "tensor"),
        P(("groups", "dp"), None, "tensor"),
        P(("groups", "dp"), None, "tensor"),
        P(("groups", "dp"), None, "tensor"),
    )
    return jax.shard_map(
        functools.partial(on_device, n_dp, nt),
        mesh=mesh, in_specs=in_specs, out_specs=out_specs, check_vma=False,
    )
```
